1024 devices in a mesh: expert: 64 (over x, y), dp: 16 (over z, core).
Axes of the slice: x: 8, y: 8, z: 8, core: 2. Of those that a mesh axis runs over, the one named last changes fastest.
Arguments:
- tokens: bfloat16 [2048, 7168], P('expert', 'dp'), may hold values from -6 to 6
- cotangent: bfloat16 [2048, 7168], P('expert', 'dp'), may hold values from -6 to 6
- expert_ids: int32 [2048, 8], P('expert'), may hold values from 0 to 63, all different within a row; in each aligned block of 32 rows (0 to 31, 32 to 63, ...) at most 8 rows name the same one
- route_weight: float32 [2048, 8], P('expert'), may hold values from 0.1 to 1
- gate_weight: bfloat16 [64, 7168, 1024], P('expert', 'dp'), may hold values from -0.0625 to 0.0625
- up_weight: bfloat16 [64, 7168, 1024], P('expert', 'dp'), may hold values from -0.0625 to 0.0625
- down_weight: bfloat16 [64, 7168, 1024], P('expert', 'dp'), may hold values from -0.1875 to 0.1875
Outputs:
- mixed: bfloat16 [2048, 7168], P('expert', 'dp')
- grad_tokens: bfloat16 [2048, 7168], P('expert', 'dp')
The draws below stay inside these ranges and needn't reach their ends.
Inputs may be any that keep to these rules, and one draw needn't show every extreme that they name: `expert_ids`: each row names 8 different experts. In the rows of one device (aligned blocks of 32 rows) no expert is named more than 8 times, and in every draw some block names some expert exactly 8 times.
All inputs are finite; a program needn't handle non-finite values.
Results may differ from the reference program's by a relative error of at most 0.028.
Values may be sent and summed in bfloat16 or wider, within the bound.
A program may use at most 32 MiB of HBM per device.

```python
import math
import jax
import jax.numpy as jnp
import numpy as np
from jax import lax

D = 7168
FF = 1024
K = 8
TOK_DEV = 32
EXPERTS = 64
CAP = 8
ROWS = 512
TOKENS = 2048
N_EXPERT = 64
N_DP = 16


def block_scale(own_key, extent, shards, smallest, top_value):
    factor_of, own = 1.0, jax.random.fold_in(own_key, 6)
    for position, shards_of in shards:
        draws = jnp.exp(jax.random.uniform(jax.random.fold_in(own, position), (shards_of,), jnp.float32, smallest / len(shards), top_value / len(shards)))
        factor_of = factor_of * jnp.repeat(draws, extent[position] // shards_of).reshape([-1 if axis == position else 1 for axis in range(len(extent))])
    return factor_of


def assign_block(key, own, number, rows, amount, top, reach, lean):
    sequence = jax.random.permutation(key, amount)
    crowded, common = portions_of(amount, rows * top, reach, lean, True), portions_of(amount, rows * top, reach, lean, False)
    places = jnp.arange(amount)

    def named(tallies, offset_by):
        used = int((tallies > 0).sum())
        fixed = max(1, used // 4)
        moved = fixed + (places - fixed + offset_by * (used - fixed)) % max(1, amount - fixed)
        return jnp.zeros((amount,), jnp.int32).at[sequence[jnp.where(places < fixed, places, moved)]].set(jnp.asarray(tallies, jnp.int32))

    tallies = jnp.where(number % 4 == 0, named(crowded, number // 4), named(common, number - number // 4 - 1))
    mixed = jax.random.permutation(jax.random.fold_in(own, 3), amount)
    donor, sink = mixed[0:amount // 2 * 2:2], mixed[1:amount // 2 * 2:2]
    slack = jnp.minimum(tallies[donor] - 1, reach - tallies[sink]) // 2
    slack = jnp.where((donor == sequence[0]) | (sink == sequence[0]) | (tallies[sink] == 0), 0, jnp.maximum(slack, 0))
    moved = jax.random.randint(jax.random.fold_in(own, 4), (amount // 2,), 0, 1 << 20) % (slack + 1)
    tallies = tallies.at[donor].add(-moved).at[sink].add(moved)
    members = jnp.searchsorted(jnp.cumsum(tallies), jnp.arange(rows * top), side="right").astype(jnp.int32)
    table = members.reshape(top, rows).T
    table = table[jax.random.permutation(jax.random.fold_in(own, 1), rows)]
    offset_by = jax.random.randint(jax.random.fold_in(own, 2), (rows, 1), 0, top)
    return jnp.take_along_axis(table, (jnp.arange(top)[None, :] + offset_by) % top, axis=1)


def portions_of(count, total, reach, lean, full):
    portions = [(1 << 20) // math.isqrt(grade ** lean) + 1 for grade in range(1, count + 1)]
    largest = reach if full else min(reach, max(-(-total // count), total * portions[0] // sum(portions)))
    least = 1 if total - largest >= count - 1 else 0
    holding, rest = [largest] + [least] * (count - 1), total - largest - least * (count - 1)
    while rest > 0:
        candidates = [i for i in range(1, count) if holding[i] < largest] or [i for i in range(1, count) if holding[i] < reach]
        whole, remaining = sum([portions[i] for i in candidates]), rest
        for i in candidates:
            extra = min(reach - holding[i], max(1, remaining * portions[i] // whole), rest)
            holding[i] = holding[i] + extra
            rest = rest - extra
    return np.array(holding)


def scatter_about(rng, dims, width, limit, cuts=(), kind=jnp.bfloat16):
    entries = width * jax.random.normal(rng, dims, jnp.float32)
    if cuts:
        entries = entries * block_scale(rng, dims, cuts, -0.22, 0.18)
    return jnp.clip(entries, -limit, limit).astype(kind)


def setup_inputs(seed: int = 0) -> dict:
    key_list = jax.random.split(jax.random.key(seed), 8)
    tokens = scatter_about(key_list[0], (TOKENS, D), 1.0, 6.0, ((0, 64), (1, 16)))
    cotangent = scatter_about(key_list[1], (TOKENS, D), 1.0, 6.0, ((0, 64), (1, 16)))
    expert_ids_keys = jax.random.split(jax.random.fold_in(key_list[2], 1), TOKENS // TOK_DEV)
    expert_ids_turns = jax.random.permutation(jax.random.fold_in(key_list[2], 3), TOKENS // TOK_DEV)
    expert_ids = jax.vmap(lambda own, number: assign_block(jax.random.fold_in(key_list[2], 2), own, number, TOK_DEV, EXPERTS, K, CAP, 2))(expert_ids_keys, expert_ids_turns).reshape((TOKENS, K))
    route_weight = jnp.clip(0.1 + 0.9 * jax.random.uniform(key_list[3], (TOKENS, K), jnp.float32) ** block_scale(key_list[3], (TOKENS, K), ((0, 64),), -0.2, 0.2), 0.1, 1.0)
    gate_weight = scatter_about(key_list[4], (EXPERTS, D, FF), D ** -0.5, 0.0625, ((0, 64), (1, 16)))
    up_weight = scatter_about(key_list[5], (EXPERTS, D, FF), D ** -0.5, 0.0625, ((0, 64), (1, 16)))
    down_weight = scatter_about(key_list[6], (EXPERTS, D, FF), FF ** -0.5, 0.1875, ((0, 64), (1, 16)))
    return {"tokens": tokens, "cotangent": cotangent, "expert_ids": expert_ids, "route_weight": route_weight, "gate_weight": gate_weight, "up_weight": up_weight, "down_weight": down_weight}


def slot_targets(ids_block):
    flat_ids = ids_block.reshape(-1)
    onehot = (flat_ids[:, None] == jnp.arange(EXPERTS, dtype=jnp.int32)[None, :]).astype(jnp.int32)
    before = jnp.cumsum(onehot, axis=0) - onehot
    return (flat_ids * CAP + jnp.sum(before * onehot, axis=1)).astype(jnp.int32)


def place_rows(target, rows):
    return jnp.zeros((EXPERTS * CAP, D), rows.dtype).at[target].set(rows)


def pick_rows(source, target):
    return source[target]


def to_experts(buffer):
    return buffer.reshape(N_EXPERT, EXPERTS, CAP, D).transpose(1, 0, 2, 3).reshape(EXPERTS, ROWS, D)


def to_blocks(buffer):
    return buffer.reshape(EXPERTS, N_EXPERT, CAP, D).transpose(1, 0, 2, 3).reshape(N_EXPERT, EXPERTS * CAP, D)


def blocked(left_rows, weight):
    share_width = D // N_DP
    partials = jnp.einsum('rnc,ncf->nrf', left_rows.reshape(ROWS, N_DP, share_width).astype(jnp.float32),
                          weight.reshape(N_DP, share_width, FF).astype(jnp.float32))
    rounded = lax.optimization_barrier(partials.astype(jnp.bfloat16))
    return jnp.sum(rounded.astype(jnp.float32), axis=0)


def expert_pass(operands):
    routed_tokens, routed_grads, gate_w, up_w, down_w = operands
    gate_pre = blocked(routed_tokens, gate_w)
    up_pre = blocked(routed_tokens, up_w)
    sig_gate = jax.nn.sigmoid(gate_pre)
    hidden = (gate_pre * sig_gate * up_pre).astype(jnp.bfloat16)
    expert_out = jnp.einsum('rf,df->rd', hidden.astype(jnp.float32), down_w.astype(jnp.float32)).astype(jnp.bfloat16)
    hidden_grad = blocked(routed_grads, down_w)
    up_grad = (hidden_grad * gate_pre * sig_gate).astype(jnp.bfloat16)
    gate_grad = (hidden_grad * up_pre * sig_gate * (1.0 + gate_pre * (1.0 - sig_gate))).astype(jnp.bfloat16)
    slot_grad = (jnp.einsum('rf,df->rd', gate_grad.astype(jnp.float32), gate_w.astype(jnp.float32))
                 + jnp.einsum('rf,df->rd', up_grad.astype(jnp.float32), up_w.astype(jnp.float32))).astype(jnp.bfloat16)
    return expert_out, slot_grad


def reference(tokens, cotangent, expert_ids, route_weight, gate_weight, up_weight, down_weight):
    pair_count = TOK_DEV * K
    targets = jax.vmap(slot_targets)(expert_ids.reshape(N_EXPERT, TOK_DEV, K))
    weights = route_weight.reshape(N_EXPERT, pair_count)
    token_rows = jnp.repeat(tokens.reshape(N_EXPERT, TOK_DEV, D), K, axis=1)
    grad_rows = (weights[:, :, None] * jnp.repeat(cotangent.reshape(N_EXPERT, TOK_DEV, D).astype(jnp.float32), K, axis=1)).astype(jnp.bfloat16)
    routed_tokens = to_experts(jax.vmap(place_rows)(targets, token_rows))
    routed_grads = to_experts(jax.vmap(place_rows)(targets, grad_rows))
    expert_out, slot_grad = lax.map(expert_pass, (routed_tokens, routed_grads, gate_weight, up_weight, down_weight))
    got_out = jax.vmap(pick_rows)(to_blocks(expert_out), targets)
    got_grad = jax.vmap(pick_rows)(to_blocks(slot_grad), targets)
    mixed = jnp.sum((weights[:, :, None] * got_out.astype(jnp.float32)).reshape(N_EXPERT, TOK_DEV, K, D), axis=2)
    grad_tokens = jnp.sum(got_grad.astype(jnp.float32).reshape(N_EXPERT, TOK_DEV, K, D), axis=2)
    return mixed.reshape(TOKENS, D).astype(jnp.bfloat16), grad_tokens.reshape(TOKENS, D).astype(jnp.bfloat16)
```

```python
import functools
import math

import jax
import jax.numpy as jnp
from jax import lax
from jax.experimental import pallas as pl
from jax.experimental.pallas import tpu as pltpu
from jax.sharding import PartitionSpec as P

MESH = pl.DeviceIdType.MESH
BF = jnp.bfloat16
F32 = jnp.float32


def dot(left, right):
    return jnp.dot(left, right, preferred_element_type=F32)


def dot_t(left, right):
    return lax.dot_general(left, right, (((1,), (1,)), ((), ())), preferred_element_type=F32)


def join(low, high, width):
    part = low.shape[1]
    edge = 2 * width - part
    lanes = lax.broadcasted_iota(jnp.int32, (low.shape[0], part - edge), 1) + edge
    middle = jnp.where(lanes < width, low[:, edge:], high[:, : part - edge])
    if edge == 0:
        return middle
    return jnp.concatenate([low[:, :edge], middle, high[:, part - edge :]], axis=1)


def kernel(
    ne, nz, top, cap, width, rows_ref, meta_ref, gate_ref, up_ref, down_ref, out_ref,
    gath, mgath, wts, keys, kw, pick, pick_hi, pick_lo, sbuf, rbuf, own, sib_out, sib_in,
    acc_a, acc_b, in_a, in_b, hid, obuf, qbuf, cbuf, fbuf,
    w_sem, m_sem, g_sem, r_sem, x_sem, ra_sem, rb_sem, ha_sem, hb_sem, hx_sem, q_sem, f_sem,
    m_snd, g_snd, r_snd, x_snd, ra_snd, rb_snd, ha_snd, hb_snd, hx_snd, q_snd, f_snd,
):
    half = nz // 2
    tok = rows_ref.shape[0]
    pad = wts.shape[1]
    low_cols, high_cols = slice(0, pad), slice(2 * width - pad, 2 * width)
    quarter = hid.shape[3]
    ff = hid.shape[4]
    e = lax.axis_index("expert")
    d = lax.axis_index("dp")
    x, y = e // ne, e % ne
    z, c = d // 2, d % 2
    a = x * (1 - c) + y * c
    b = y * (1 - c) + x * c
    step_a = ne - c * (ne - 1)
    step_b = 1 + c * (ne - 1)
    sign = 1 - 2 * c

    def place(aa, bb):
        return (aa * step_a + bb * step_b, d)

    side = (e, z * 2 + (1 - c))
    next_a = (e, ((z + sign + nz) % nz) * 2 + c)
    next_b = (e, ((z - sign + nz) % nz) * 2 + c)

    def remote(src, dst, send, recv, device):
        pltpu.make_async_remote_copy(
            src_ref=src, dst_ref=dst, send_sem=send, recv_sem=recv, device_id=device, device_id_type=MESH
        ).start()

    def wait(ref, sem):
        pltpu.make_async_copy(ref, ref, sem).wait()

    loads = [
        pltpu.make_async_copy(gate_ref, wts.at[0, pl.ds(0, width)], w_sem.at[0]),
        pltpu.make_async_copy(up_ref, wts.at[1, pl.ds(0, width)], w_sem.at[1]),
        pltpu.make_async_copy(down_ref, wts.at[2, pl.ds(pad - width, width)], w_sem.at[2]),
    ]
    for load in loads:
        load.start()

    barrier = pltpu.get_barrier_semaphore()
    greeted = [place((a + p) % ne, b) for p in range(1, ne)] + [place(a, (b + p) % ne) for p in range(1, ne)]
    greeted += [side, next_a, next_b]
    for device in greeted:
        pl.semaphore_signal(barrier, inc=1, device_id=device, device_id_type=MESH)
    if pad > width:
        blank = jnp.zeros((pad - width, ff), BF)
        wts[0, width:] = blank
        wts[1, width:] = blank
        wts[2, : pad - width] = blank
    pl.semaphore_wait(barrier, len(greeted))

    peers = sorted(range(1, ne), key=lambda p: -min(p, ne - p))
    for p in peers:
        remote(meta_ref, mgath.at[a], m_snd, m_sem, place((a + p) % ne, b))
    pltpu.make_async_copy(meta_ref, mgath.at[a], m_sem).start()
    for p in peers:
        remote(rows_ref, gath.at[a], g_snd, g_sem, place((a + p) % ne, b))
    pltpu.make_async_copy(rows_ref, gath.at[a], g_sem).start()

    wait(mgath, m_sem)
    lanes = mgath.shape[2]
    per = lanes // tok
    lane = lax.broadcasted_iota(jnp.int32, (2 * top, lanes), 1)
    parts = []
    for first in range(0, ne, per):
        total = jnp.zeros((2 * top, lanes), F32)
        for i in range(min(per, ne - first)):
            total = total + jnp.where(lane // tok == i, mgath[first + i], 0.0)
        parts.append(total)
    merged = jnp.concatenate(parts, axis=1) if len(parts) > 1 else parts[0]
    span = merged.shape[1]
    ids, weight = merged[:top], merged[top:]
    named, carried = [], []
    for i in range(ne):
        same = ids == (a * step_a + i * step_b).astype(F32)
        named.append(jnp.sum(same.astype(F32), axis=0, keepdims=True))
        carried.append(jnp.sum(jnp.where(same, weight, 0.0), axis=0, keepdims=True))
    named = jnp.concatenate(named, axis=0)
    row = lax.broadcasted_iota(jnp.int32, (span, span), 0)
    col = lax.broadcasted_iota(jnp.int32, (span, span), 1)
    earlier = ((row // tok == col // tok) & (row < col)).astype(F32).astype(BF)
    slot = dot(named.astype(BF), earlier)
    keys[...] = jnp.where(named > 0.5, slot, -1.0)
    kw[...] = jnp.concatenate(carried, axis=0)

    def choose(i, carry):
        row = lax.broadcasted_iota(jnp.int32, (ne * cap, span), 0)
        col = lax.broadcasted_iota(jnp.int32, (ne * cap, span), 1)
        hit = (keys[pl.ds(i, 1)] == (row % cap).astype(F32)) & (row // cap == col // tok)
        scaled = jnp.where(hit, kw[pl.ds(i, 1)], 0.0)
        high = scaled.astype(BF)
        at = pl.ds(pl.multiple_of(i * (ne * cap), ne * cap), ne * cap)
        pick[at] = hit.astype(F32).astype(BF)
        pick_hi[at] = high
        pick_lo[at] = (scaled - high.astype(F32)).astype(BF)
        return carry

    lax.fori_loop(0, ne, choose, 0)

    wait(gath, g_sem)

    def route(i, carry):
        at = pl.ds(pl.multiple_of(i * (ne * cap), ne * cap), ne * cap)
        source = gath[...].reshape(ne * tok, 2 * width)
        low = dot(pick[at], source[:, low_cols])
        high = dot(pick_hi[at], source[:, high_cols]) + dot(pick_lo[at], source[:, high_cols])
        sbuf[i] = join(low, high, width).reshape(ne, cap, 2 * width).astype(BF)
        return carry

    lax.fori_loop(0, ne, route, 0)

    def chunk(i):
        off = (half - (i + 1) // 2) * (2 * (i % 2) - 1)
        return (z + off + nz) % nz

    def dispatch(i, carry):
        j = chunk(i)

        @pl.when(c == 0)
        def _():
            to = (b - j + ne) % ne

            @pl.when(j == 0)
            def _():
                pltpu.make_async_copy(sbuf.at[b], rbuf.at[0], r_sem.at[0]).start()

            @pl.when(j != 0)
            def _():
                remote(sbuf.at[to], rbuf.at[j], r_snd, r_sem.at[j], place(a, to))

        @pl.when(c == 1)
        def _():
            of = (a + j) % ne
            for p in peers:
                to = (b + p) % ne
                remote(sbuf.at[to, of], rbuf.at[j, b], r_snd, r_sem.at[j], place(a, to))
            pltpu.make_async_copy(sbuf.at[b, of], rbuf.at[j, b], r_sem.at[j]).start()

        return carry

    lax.fori_loop(0, nz, dispatch, 0)
    for load in loads:
        load.wait()

    def forward(i, carry):
        j = chunk(i)
        wait(rbuf.at[j], r_sem.at[j])
        rows = rbuf[j].astype(F32).reshape(ne * cap, 2 * width)
        rows_low = rows[:, low_cols].astype(BF)
        rows_high = rows[:, high_cols].astype(BF)
        for p in range(3):
            part = dot(rows_low if p < 2 else rows_high, wts[p])
            first, second = part[:quarter], part[quarter:]
            swap = jnp.broadcast_to(c, first.shape) == 1
            own[p, j] = jnp.where(swap, second, first)
            sib_out[p, j] = jnp.where(swap, first, second).astype(BF)
            remote(sib_out.at[p, j], sib_in.at[p, j], x_snd, x_sem.at[p, j], side)
        return carry

    def both(p, j):
        wait(sib_in.at[p, j], x_sem.at[p, j])
        return own[p, j] + sib_in[p, j].astype(F32)

    lax.fori_loop(0, 3, forward, 0)
    done = 3
    for m in range(half):
        for p in range(3):
            value = both(p, (z + sign * (half - m) + nz) % nz)
            if m > 0:
                wait(in_a.at[m - 1, p], ra_sem.at[m - 1, p])
                value = value + in_a[m - 1, p].astype(F32)
            acc_a[m, p] = value.astype(BF)
            remote(acc_a.at[m, p], in_a.at[m, p], ra_snd, ra_sem.at[m, p], next_a)
            if m < half - 1:
                value = both(p, (z - sign * (half - 1 - m) + nz) % nz)
                if m > 0:
                    wait(in_b.at[m - 1, p], rb_sem.at[m - 1, p])
                    value = value + in_b[m - 1, p].astype(F32)
                acc_b[m, p] = value.astype(BF)
                remote(acc_b.at[m, p], in_b.at[m, p], rb_snd, rb_sem.at[m, p], next_b)
        more = min(nz, done + 2)
        if more > done:
            lax.fori_loop(done, more, forward, 0)
        done = more

    for p in range(3):
        wait(sib_in.at[p, z], x_sem.at[p, z])
        wait(in_b.at[half - 2, p], rb_sem.at[half - 2, p])
        wait(in_a.at[half - 1, p], ra_sem.at[half - 1, p])

    def activate(q, carry):
        at = pl.ds(pl.multiple_of(q * 128, 128), 128)

        def total(p):
            value = own[p, z, :, at] + sib_in[p, z, :, at].astype(F32)
            return value + in_a[half - 1, p, :, at].astype(F32) + in_b[half - 2, p, :, at].astype(F32)

        gate, up, grad = total(0), total(1), total(2)
        sig = jax.nn.sigmoid(gate)
        hid[0, z, c, :, at] = (gate * sig * up).astype(BF)
        hid[1, z, c, :, at] = (grad * up * sig * (1.0 + gate * (1.0 - sig))).astype(BF)
        hid[2, z, c, :, at] = (grad * gate * sig).astype(BF)
        return carry

    lax.fori_loop(0, ff // 128, activate, 0)

    def share(p, j):
        remote(hid.at[p, j, c], hid.at[p, j, c], hx_snd, hx_sem.at[p, j], side)

    def backward(j):
        for p in range(3):
            wait(hid.at[p, j, 1 - c], hx_sem.at[p, j])
        acts = [hid[p, j].reshape(2 * quarter, ff) for p in range(3)]
        low = dot_t(acts[1], wts[0]) + dot_t(acts[2], wts[1])
        high = dot_t(acts[0], wts[2])
        obuf[j] = join(low, high, width).reshape(ne, cap, 2 * width).astype(BF)

        @pl.when(c == 0)
        def _():
            to = (b + j) % ne

            @pl.when(j == 0)
            def _():
                pltpu.make_async_copy(obuf.at[0], qbuf.at[b], q_sem).start()

            @pl.when(j != 0)
            def _():
                remote(obuf.at[j], qbuf.at[b], q_snd, q_sem, place(a, to))

        @pl.when(c == 1)
        def _():
            of = (a + j) % ne
            for p in peers:
                to = (b + p) % ne
                remote(obuf.at[j, to], qbuf.at[b, of], q_snd, q_sem, place(a, to))
            pltpu.make_async_copy(obuf.at[j, b], qbuf.at[b, of], q_sem).start()

    for p in range(3):
        remote(hid.at[p, z, c], hid.at[p, z, c], ha_snd, ha_sem.at[0, p], next_a)
        remote(hid.at[p, z, c], hid.at[p, z, c], hb_snd, hb_sem.at[0, p], next_b)
        share(p, z)
    for k in range(1, half + 1):
        for p in range(3):
            j = (z - sign * k + nz) % nz
            wait(hid.at[p, j, c], ha_sem.at[k - 1, p])
            if k < half:
                remote(hid.at[p, j, c], hid.at[p, j, c], ha_snd, ha_sem.at[k, p], next_a)
            share(p, j)
            if k < half:
                j = (z + sign * k + nz) % nz
                wait(hid.at[p, j, c], hb_sem.at[k - 1, p])
                if k < half - 1:
                    remote(hid.at[p, j, c], hid.at[p, j, c], hb_snd, hb_sem.at[k, p], next_b)
                share(p, j)
        if k == 1:
            backward(z)
        else:

            def pair(i, carry, k=k):
                backward((z + (k - 1) * (1 - 2 * i) + nz) % nz)
                return carry

            lax.fori_loop(0, 2, pair, 0)
    backward((z + half) % nz)

    wait(qbuf, q_sem)
    back = qbuf[...].astype(F32).reshape(ne * ne * cap, 2 * width)
    across = (((0,), (0,)), ((), ()))
    back_low, back_high = back[:, low_cols].astype(BF), back[:, high_cols].astype(BF)
    low = lax.dot_general(pick[...], back_low, across, preferred_element_type=F32)
    high = lax.dot_general(pick_hi[...], back_high, across, preferred_element_type=F32)
    high = high + lax.dot_general(pick_lo[...], back_high, across, preferred_element_type=F32)
    cbuf[...] = join(low, high, width).astype(BF).reshape(ne, tok, 2 * width)
    for p in peers:
        to = (a + p) % ne
        remote(cbuf.at[to], fbuf.at[a], f_snd, f_sem, place(to, b))
    pltpu.make_async_copy(cbuf.at[a], fbuf.at[a], f_sem).start()
    wait(fbuf, f_sem)
    total = fbuf[0].astype(F32)
    for i in range(1, ne):
        total = total + fbuf[i].astype(F32)
    out_ref[...] = total.astype(BF)

    wait(mgath.at[pl.ds(0, ne - 1)], m_snd)
    wait(gath.at[pl.ds(0, ne - 1)], g_snd)
    wait(sbuf.at[pl.ds(0, ne - 1)], r_snd)
    wait(obuf.at[pl.ds(0, nz - 1)], q_snd)
    wait(cbuf.at[pl.ds(0, ne - 1)], f_snd)
    wait(sib_out, x_snd)
    wait(acc_a, ra_snd)
    wait(acc_b, rb_snd)
    wait(hid.at[:, pl.ds(0, half), 0], ha_snd)
    wait(hid.at[:, pl.ds(0, half - 1), 0], hb_snd)
    wait(hid.at[:, :, 0], hx_snd)


def local(ne, nz, tokens, cotangent, expert_ids, route_weight, gate_weight, up_weight, down_weight):
    tok, width = tokens.shape
    top = expert_ids.shape[1]
    ff = gate_weight.shape[2]
    cap = max(2, min(tok, 2 * tok * top // (ne * ne)))
    pad = -(-width // 128) * 128
    quarter = ne * cap // 2
    rows = jnp.concatenate([tokens, cotangent], axis=1)
    meta = jnp.concatenate([expert_ids.astype(F32), route_weight], axis=1).T
    meta = jnp.tile(meta, (1, 128 // tok))
    span = -(-ne // (128 // tok)) * 128
    half = nz // 2
    dma = pltpu.SemaphoreType.DMA
    scratch = [
        pltpu.VMEM((ne, tok, 2 * width), BF),
        pltpu.VMEM((ne, 2 * top, 128), F32),
        pltpu.VMEM((3, pad, ff), BF),
        pltpu.VMEM((ne, span), F32),
        pltpu.VMEM((ne, span), F32),
        pltpu.VMEM((ne * ne * cap, span), BF),
        pltpu.VMEM((ne * ne * cap, span), BF),
        pltpu.VMEM((ne * ne * cap, span), BF),
        pltpu.VMEM((ne, ne, cap, 2 * width), BF),
        pltpu.VMEM((nz, ne, cap, 2 * width), BF),
        pltpu.VMEM((3, nz, quarter, ff), F32),
        pltpu.VMEM((3, nz, quarter, ff), BF),
        pltpu.VMEM((3, nz, quarter, ff), BF),
        pltpu.VMEM((half, 3, quarter, ff), BF),
        pltpu.VMEM((half - 1, 3, quarter, ff), BF),
        pltpu.VMEM((half, 3, quarter, ff), BF),
        pltpu.VMEM((half - 1, 3, quarter, ff), BF),
        pltpu.VMEM((3, nz, 2, quarter, ff), BF),
        pltpu.VMEM((nz, ne, cap, 2 * width), BF),
        pltpu.VMEM((ne, ne, cap, 2 * width), BF),
        pltpu.VMEM((ne, tok, 2 * width), BF),
        pltpu.VMEM((ne, tok, 2 * width), BF),
        dma((3,)),
        dma,
        dma,
        dma((nz,)),
        dma((3, nz)),
        dma((half, 3)),
        dma((half - 1, 3)),
        dma((half, 3)),
        dma((half - 1, 3)),
        dma((3, nz)),
        dma,
        dma,
    ] + [dma] * 11
    vmem, anywhere = pl.BlockSpec(memory_space=pltpu.VMEM), pl.BlockSpec(memory_space=pl.ANY)
    out = pl.pallas_call(
        functools.partial(kernel, ne, nz, top, cap, width),
        out_shape=jax.ShapeDtypeStruct((tok, 2 * width), BF),
        in_specs=[vmem, vmem, anywhere, anywhere, anywhere],
        out_specs=vmem,
        scratch_shapes=scratch,
        compiler_params=pltpu.CompilerParams(
            collective_id=0, has_side_effects=True, vmem_limit_bytes=50 * 2**20
        ),
    )(rows, meta, gate_weight[0], up_weight[0], down_weight[0])
    return out[:, width:], out[:, :width]


def solution(mesh):
    ne = math.isqrt(mesh.shape["expert"])
    nz = mesh.shape["dp"] // 2
    return jax.shard_map(
        functools.partial(local, ne, nz),
        mesh=mesh,
        in_specs=(
            P("expert", "dp"),
            P("expert", "dp"),
            P("expert", None),
            P("expert", None),
            P("expert", "dp", None),
            P("expert", "dp", None),
            P("expert", "dp", None),
        ),
        out_specs=(P("expert", "dp"), P("expert", "dp")),
        check_vma=False,
    )
```
